128 devices in a mesh: frames: 32 (over z, x, core), rows: 4 (over y).
Axes of the slice: x: 4, y: 4, z: 4, core: 2. Of those that a mesh axis runs over, the one named last changes fastest.
Arguments:
- acts: bfloat16 [128, 12, 256, 256], P('frames', 'rows'), may hold values from -6 to 6
- grad_out: bfloat16 [128, 12, 256, 256], P('frames', 'rows'), may hold values from -6 to 6
- kernel: bfloat16 [3, 3, 3, 256, 256], replicated, may hold values from -0.078125 to 0.078125
Outputs:
- grad_acts: bfloat16 [128, 12, 256, 256], P('frames', 'rows')
- weight_grad: float32 [3, 3, 3, 256, 256], replicated
The draws below stay inside these ranges and needn't reach their ends.
All inputs are finite; a program needn't handle non-finite values.
Results may differ from the reference program's by a relative error of at most 0.0031.
Values may be sent and summed in bfloat16 or wider, within the bound.
A program may use at most 256 MiB of HBM per device.

```python
import math
import jax
import jax.numpy as jnp

CH = 256
WIDTH = 256
TF = 128
HEIGHT = 12


def levels(key, extent, shards, smallest, largest):
    factor_of, own = 1.0, jax.random.fold_in(key, 6)
    for axis_at, parts in shards:
        steps = jnp.exp(jax.random.uniform(jax.random.fold_in(own, axis_at), (parts,), jnp.float32, smallest / len(shards), largest / len(shards)))
        factor_of = factor_of * jnp.repeat(steps, extent[axis_at] // parts).reshape([-1 if axis == axis_at else 1 for axis in range(len(extent))])
    return factor_of


def scatter_about(stream_key, extent, width, most, cuts=(), kind=jnp.bfloat16):
    gain = levels(stream_key, extent, cuts, -0.22, 0.18) if cuts else 1.0
    result = jax.random.normal(stream_key, extent, jnp.float32) * width * gain
    return jnp.minimum(jnp.maximum(result, -most), most).astype(kind)


def setup_inputs(seed: int = 0) -> dict:
    streams_of = jax.random.split(jax.random.key(seed), 4)
    return {
        "acts": scatter_about(streams_of[0], (TF, HEIGHT, CH, WIDTH), 1.0, 6.0, ((0, 32), (1, 4))),
        "grad_out": scatter_about(streams_of[1], (TF, HEIGHT, CH, WIDTH), 1.0, 6.0, ((0, 32), (1, 4))),
        "kernel": scatter_about(streams_of[2], (3, 3, 3, CH, CH), (27 * CH) ** -0.5, 0.078125),
    }


def reference(acts, grad_out, kernel):
    x32 = acts.astype(jnp.float32)
    sig = jax.nn.sigmoid(x32)
    activ = (x32 * sig).astype(jnp.bfloat16).astype(jnp.float32)
    grad32 = grad_out.astype(jnp.float32)
    padded = jnp.pad(grad32, ((0, 2), (1, 1), (0, 0), (1, 1)))
    k32 = kernel.astype(jnp.float32)
    grad_activ = jnp.zeros(x32.shape, jnp.float32)
    pieces = []
    for kt in range(3):
        for kh in range(3):
            for kw in range(3):
                piece = padded[2 - kt:2 - kt + TF, 2 - kh:2 - kh + HEIGHT, :, 2 - kw:2 - kw + WIDTH]
                grad_activ = grad_activ + jnp.einsum('thow,io->thiw', piece, k32[kt, kh, kw])
                pieces.append(jnp.einsum('thiw,thow->io', activ, piece))
    grad_acts = (grad_activ * sig * (1.0 + x32 * (1.0 - sig))).astype(jnp.bfloat16)
    scale = 1.0 / math.sqrt(TF * HEIGHT * WIDTH)
    weight_grad = jnp.stack(pieces).reshape(3, 3, 3, CH, CH) * scale
    return (grad_acts, weight_grad)
```

```python
import functools
import math

import jax
import jax.numpy as jnp
from jax import lax
from jax.experimental import pallas as pl
from jax.experimental.pallas import tpu as pltpu
from jax.sharding import PartitionSpec as P

MESH = pl.DeviceIdType.MESH
BF16, F32 = jnp.bfloat16, jnp.float32
AXES = "xyz"


def place():
    f = lax.axis_index("frames")
    return {"core": f % 2, "x": (f // 2) % 4, "z": f // 8, "y": lax.axis_index("rows")}


def device(at):
    return (at["z"] * 8 + at["x"] * 2 + at["core"], at["y"])


def moved(at, axis, steps):
    there = dict(at)
    size = 2 if axis == "core" else 4
    there[axis] = (at[axis] + steps + size) % size
    return device(there)


def body(
    acts_hbm, grad_hbm, kern_hbm, gacts_hbm, wsum_hbm,
    acts, g, k, a3, slope, w, cacc, gout, r0, s1, r1, s2, r2, s3, r3, w16,
    local_sem, halo_send, halo_recv, pair_send, pair_recv, ring_send, ring_recv,
):
    at = place()
    c = at["core"]
    f, r = lax.axis_index("frames"), lax.axis_index("rows")
    f_prev, f_next = (f + 31) % 32, (f + 1) % 32
    r_prev, r_next = (r + 3) % 4, (r + 1) % 4
    partner = moved(at, "core", 1)

    loads = [
        pltpu.make_async_copy(acts_hbm, acts, local_sem.at[0]),
        pltpu.make_async_copy(grad_hbm, g.at[pl.ds(0, 4), pl.ds(1, 3)], local_sem.at[1]),
        pltpu.make_async_copy(kern_hbm, k, local_sem.at[2]),
    ]
    for load in loads:
        load.start()

    barrier = pltpu.get_barrier_semaphore()
    peers = [partner, (f_prev, r), (f_next, r)]
    peers += [moved(at, axis, d) for axis in AXES for d in (1, 2, 3)]
    for peer in peers:
        pl.semaphore_signal(barrier, inc=1, device_id=peer, device_id_type=MESH)
    pl.semaphore_wait(barrier, len(peers))

    def remote(src, dst, ssem, rsem, to):
        return pltpu.make_async_remote_copy(
            src_ref=src, dst_ref=dst, send_sem=ssem, recv_sem=rsem,
            device_id=to, device_id_type=MESH,
        )

    def halo(n, src, dst, to):
        return remote(src, dst, halo_send.at[n], halo_recv.at[n], to)

    early, late, beyond = pl.ds(0, 2), pl.ds(2, 2), pl.ds(4, 2)
    halos = [
        halo(0, grad_hbm.at[early, 2], g.at[early, 0], (f, r_next)),
        halo(1, grad_hbm.at[early, 0], g.at[early, 4], (f, r_prev)),
        halo(2, grad_hbm.at[early], g.at[beyond, pl.ds(1, 3)], (f_prev, r)),
        halo(3, grad_hbm.at[late, 2], g.at[late, 0], (f, r_next)),
        halo(4, grad_hbm.at[late, 0], g.at[late, 4], (f, r_prev)),
        halo(5, g.at[early, 0], g.at[beyond, 0], (f_prev, r)),
        halo(6, g.at[early, 4], g.at[beyond, 4], (f_prev, r)),
    ]
    for copy in halos[:5]:
        copy.start()

    loads[0].wait()
    lane = lax.broadcasted_iota(jnp.int32, (256, 256), 1)

    @pl.loop(0, 12)
    def _(n):
        t, h = n // 3, n % 3
        x = acts[t, h].astype(F32)
        sig = jax.nn.sigmoid(x)
        activ = (x * sig).astype(BF16)
        slope[t, h] = sig * (1.0 + x * (1.0 - sig))
        wide = activ.astype(F32)
        a3[t, h, 1] = activ
        a3[t, h, 0] = jnp.where(lane == 0, 0.0, pltpu.roll(wide, 1, 1)).astype(BF16)
        a3[t, h, 2] = jnp.where(lane == 255, 0.0, pltpu.roll(wide, 255, 1)).astype(BF16)

    def weight_part(kt, kh, t, hs, write=False):
        acc = None if write else w[kt * 3 + kh].reshape(768, 256)
        for h in hs:
            term = lax.dot_general(
                a3[t, h].reshape(768, 256), g[t + 2 - kt, h + 2 - kh],
                (((1,), (1,)), ((), ())), preferred_element_type=F32,
            )
            acc = term if acc is None else acc + term
        w[kt * 3 + kh] = acc.reshape(3, 256, 256)

    def input_part(kt, t, h, khs, write=False):
        acc = None if write else cacc[t, h]
        for kh in khs:
            term = jnp.dot(
                k[kt, kh].reshape(768, 256), g[t + 2 - kt, h + 2 - kh],
                preferred_element_type=F32,
            )
            acc = term if acc is None else acc + term
        cacc[t, h] = acc

    inner_h = {0: (0, 1), 1: (0, 1, 2), 2: (1, 2)}
    inner_kh = {0: (0, 1), 1: (0, 1, 2), 2: (1, 2)}

    loads[1].wait()

    @pl.loop(0, 3)
    def _(kt):
        for kh in range(3):
            weight_part(kt, kh, 0, inner_h[kh], write=True)

        @pl.loop(1, kt + 2)
        def _(t):
            for kh in range(3):
                weight_part(kt, kh, t, inner_h[kh])

    loads[2].wait()

    @pl.loop(0, 4)
    def _(t):
        for h in range(3):
            input_part(2, t, h, inner_kh[h], write=True)

        @pl.loop(jnp.maximum(t - 1, 0), 2)
        def _(kt):
            for h in range(3):
                input_part(kt, t, h, inner_kh[h])

    def clear(frames, row):
        for t in frames:
            g[t, row] = jnp.zeros((256, 256), BF16)

    def edge_rows(frames):
        @pl.when(r == 0)
        def _():
            clear(frames, 0)

        @pl.when(r == 3)
        def _():
            clear(frames, 4)

    halos[0].wait_recv()
    halos[1].wait_recv()
    edge_rows((0, 1))
    halos[5].start()
    halos[6].start()
    halos[3].wait_recv()
    halos[4].wait_recv()
    edge_rows((2, 3))

    def pair_sum(kt):
        return remote(
            w.at[pl.ds(3 * kt, 3), :, pl.ds(pl.multiple_of(128 * (1 - c), 128), 128)],
            r0.at[kt], pair_send.at[kt], pair_recv.at[kt], partner,
        )

    def pair_gather(kt, half):
        part = w16.at[pl.ds(3 * kt, 3), :, pl.ds(pl.multiple_of(128 * half, 128), 128)]
        return remote(part, part, pair_send.at[3 + kt], pair_recv.at[3 + kt], partner)

    def ring(stage, kt, kw, d, src, dst, axis):
        n = ((stage * 3 + kt) * 3 + kw) * 3 + d
        return remote(src, dst, ring_send.at[n], ring_recv.at[n], moved(at, axis, d + 1))

    def order(kw):
        return AXES[kw], AXES[(kw + 1) % 3], AXES[(kw + 2) % 3]

    def tile(p):
        return (
            pl.ds(pl.multiple_of(16 * (p // 2), 16), 16),
            pl.ds(pl.multiple_of(128 * (p % 2), 128), 128),
        )

    def rows32(p):
        return pl.ds(pl.multiple_of(32 * p, 32), 32)

    def scatter_one(kt, kw, d):
        first = order(kw)[0]
        to = (at[first] + d + 1) % 4
        return ring(0, kt, kw, d, s1.at[kt, kw, :, rows32(to)], r1.at[kt, kw, d], first)

    def scatter_two(kt, kw, d):
        second = order(kw)[1]
        rows, cols = tile((at[second] + d + 1) % 4)
        return ring(1, kt, kw, d, s2.at[kt, kw, :, rows, cols], r2.at[kt, kw, d], second)

    def sum_three(kt, kw, d):
        return ring(2, kt, kw, d, s3.at[kt, kw], r3.at[kt, kw, d], order(kw)[2])

    def gather_two(kt, kw, d, back=0):
        first, second, _ = order(kw)
        rows, cols = tile((at[second] + 4 - back) % 4)
        rows = pl.ds(
            pl.multiple_of(128 * c + 32 * at[first] + 16 * (((at[second] + 4 - back) % 4) // 2), 16), 16
        )
        part = w16.at[pl.ds(3 * kt, 3), kw, rows, cols]
        return ring(3, kt, kw, d, part, part, second)

    def gather_one(kt, kw, d, back=0):
        first = order(kw)[0]
        part = w16.at[
            pl.ds(3 * kt, 3), kw,
            pl.ds(pl.multiple_of(128 * c + 32 * ((at[first] + 4 - back) % 4), 32), 32),
        ]
        return ring(4, kt, kw, d, part, part, first)

    def start_pair(kt):
        pair_sum(kt).start()

    def start_one(kt):
        pair_sum(kt).wait_recv()
        mine = pl.ds(pl.multiple_of(128 * c, 128), 128)
        for kw in range(3):
            for kh in range(3):
                s1[kt, kw, kh] = (w[3 * kt + kh, kw, mine] + r0[kt, kh, kw]).astype(BF16)
            for d in range(3):
                scatter_one(kt, kw, d).start()

    def start_two(kt):
        for kw in range(3):
            p = at[order(kw)[0]]
            for d in range(3):
                scatter_one(kt, kw, d).wait_recv()
            own = pl.ds(pl.multiple_of(128 * c + 32 * p, 32), 32)
            for kh in range(3):
                total = w[3 * kt + kh, kw, own] + r0[kt, kh, kw, rows32(p)]
                for d in range(3):
                    total = total + r1[kt, kw, d, kh].astype(F32)
                s2[kt, kw, kh] = total
            for d in range(3):
                scatter_two(kt, kw, d).start()

    def start_three(kt):
        for kw in range(3):
            rows, cols = tile(at[order(kw)[1]])
            for d in range(3):
                scatter_two(kt, kw, d).wait_recv()
            total = s2[kt, kw, :, rows, cols]
            for d in range(3):
                total = total + r2[kt, kw, d]
            s3[kt, kw] = total
            for d in range(3):
                sum_three(kt, kw, d).start()

    def start_gather_two(kt):
        for kw in range(3):
            first, second, _ = order(kw)
            rows, cols = tile(at[second])
            for d in range(3):
                sum_three(kt, kw, d).wait_recv()
            total = (s3[kt, kw] + r3[kt, kw, 1]) + (r3[kt, kw, 0] + r3[kt, kw, 2])
            rows = pl.ds(pl.multiple_of(128 * c + 32 * at[first] + 16 * (at[second] // 2), 16), 16)
            w16[pl.ds(3 * kt, 3), kw, rows, cols] = total.astype(BF16)
            for d in range(3):
                gather_two(kt, kw, d).start()

    def start_gather_one(kt):
        for kw in range(3):
            for d in range(3):
                gather_two(kt, kw, d, d + 1).wait_recv()
            for d in range(3):
                gather_one(kt, kw, d).start()

    def start_pair_gather(kt):
        for kw in range(3):
            for d in range(3):
                gather_one(kt, kw, d, d + 1).wait_recv()
        pair_gather(kt, c).start()

    def write_out(kt):
        part = pl.ds(3 * kt, 3)
        return pltpu.make_async_copy(w16.at[part], wsum_hbm.at[part], local_sem.at[4 + kt])

    def finish(kt):
        pair_gather(kt, 1 - c).wait_recv()
        write_out(kt).start()

    def edge_weights(kt):
        @pl.loop(0, kt + 2)
        def _(t):
            weight_part(kt, 0, t, (2,))
            weight_part(kt, 2, t, (0,))

    edge_weights(2)
    start_pair(2)
    edge_weights(1)
    start_one(2)
    edge_weights(0)

    halos[2].wait_recv()
    halos[5].wait_recv()
    halos[6].wait_recv()

    @pl.when(f == 31)
    def _():
        for row in range(5):
            clear((4, 5), row)

    for kh in range(3):
        weight_part(1, kh, 3, (0, 1, 2))
    start_pair(1)
    start_two(2)

    @pl.loop(2, 4)
    def _(t):
        for kh in range(3):
            weight_part(0, kh, t, (0, 1, 2))

    start_pair(0)
    start_one(1)
    start_three(2)

    def finish_input(t):
        for h in range(3):
            y = cacc[t, h]
            left = jnp.where(lane == 255, 0.0, pltpu.roll(y[:256], 255, 1))
            right = jnp.where(lane == 0, 0.0, pltpu.roll(y[512:], 1, 1))
            gout[t, h] = ((y[256:512] + left + right) * slope[t, h]).astype(BF16)

    def edge_inputs(t):
        @pl.loop(max(t - 1, 0), 3)
        def _(kt):
            input_part(kt, t, 0, (2,))
            input_part(kt, t, 2, (0,))

        @pl.loop(0, max(t - 1, 0))
        def _(kt):
            for h in range(3):
                input_part(kt, t, h, (0, 1, 2))

        finish_input(t)

    edge_inputs(0)
    start_one(0)
    start_two(1)
    start_gather_two(2)
    edge_inputs(1)
    start_two(0)
    start_three(1)
    start_gather_one(2)
    edge_inputs(2)
    start_three(0)
    start_gather_two(1)
    start_pair_gather(2)
    edge_inputs(3)
    result = pltpu.make_async_copy(gout, gacts_hbm, local_sem.at[3])
    result.start()
    start_gather_two(0)
    start_gather_one(1)
    finish(2)
    start_gather_one(0)
    start_pair_gather(1)
    start_pair_gather(0)
    finish(1)
    finish(0)

    result.wait()
    for copy in halos:
        copy.wait_send()
    for kt in range(3):
        write_out(kt).wait()
        pair_sum(kt).wait_send()
        pair_gather(kt, c).wait_send()
        for kw in range(3):
            for d in range(3):
                for step in (scatter_one, scatter_two, sum_three, gather_two, gather_one):
                    step(kt, kw, d).wait_send()


def fused(acts, grad_out, kernel):
    flops = 4 * 27 * 256 * 256 * 3072
    dma = pltpu.SemaphoreType.DMA
    return pl.pallas_call(
        body,
        out_shape=(
            jax.ShapeDtypeStruct(acts.shape, BF16),
            jax.ShapeDtypeStruct((9, 3, 256, 256), BF16),
        ),
        in_specs=[pl.BlockSpec(memory_space=pl.ANY)] * 3,
        out_specs=(pl.BlockSpec(memory_space=pl.ANY),) * 2,
        scratch_shapes=[
            pltpu.VMEM((4, 3, 256, 256), BF16),
            pltpu.VMEM((6, 5, 256, 256), BF16),
            pltpu.VMEM((3, 3, 3, 256, 256), BF16),
            pltpu.VMEM((4, 3, 3, 256, 256), BF16),
            pltpu.VMEM((4, 3, 256, 256), F32),
            pltpu.VMEM((9, 3, 256, 256), F32),
            pltpu.VMEM((4, 3, 768, 256), F32),
            pltpu.VMEM((4, 3, 256, 256), BF16),
            pltpu.VMEM((3, 3, 3, 128, 256), F32),
            pltpu.VMEM((3, 3, 3, 128, 256), BF16),
            pltpu.VMEM((3, 3, 3, 3, 32, 256), BF16),
            pltpu.VMEM((3, 3, 3, 32, 256), F32),
            pltpu.VMEM((3, 3, 3, 3, 16, 128), F32),
            pltpu.VMEM((3, 3, 3, 16, 128), F32),
            pltpu.VMEM((3, 3, 3, 3, 16, 128), F32),
            pltpu.VMEM((9, 3, 256, 256), BF16),
            dma((7,)),
            dma((7,)),
            dma((7,)),
            dma((6,)),
            dma((6,)),
            dma((135,)),
            dma((135,)),
        ],
        compiler_params=pltpu.CompilerParams(
            collective_id=0, has_side_effects=True, vmem_limit_bytes=60 * 2**20
        ),
        cost_estimate=pl.CostEstimate(flops=flops, bytes_accessed=16_000_000, transcendentals=0),
        name="conv_grads",
    )(acts, grad_out, kernel)


def on_device(acts, grad_out, kernel):
    cells = 1
    for dim, axis in ((0, "frames"), (1, "rows")):
        cells *= acts.shape[dim] * lax.axis_size(axis)
    cells *= acts.shape[3]
    grad_acts, total = fused(acts, grad_out, kernel)
    weight_grad = total.astype(F32).reshape(kernel.shape) * (1.0 / math.sqrt(cells))
    return (grad_acts, weight_grad)


def solution(mesh):
    placed = (P("frames", "rows", None, None), P("frames", "rows", None, None), P())
    return jax.shard_map(
        on_device,
        mesh=mesh,
        in_specs=placed,
        out_specs=(P("frames", "rows", None, None), P()),
        check_vma=False,
    )
```

```python
import functools
import math

import jax
import jax.numpy as jnp
from jax import lax
from jax.experimental import pallas as pl
from jax.experimental.pallas import tpu as pltpu
from jax.sharding import PartitionSpec as P

MESH = pl.DeviceIdType.MESH
BF16, F32 = jnp.bfloat16, jnp.float32
AXES = "xyz"
TAPS = ((2, 1), (1, 1), (0, 1), (2, 0), (2, 2), (1, 0), (1, 2), (0, 0), (0, 2))
BATCHES = ((0, 3), (3, 2), (5, 2), (7, 2))


def place():
    f = lax.axis_index("frames")
    return {"core": f % 2, "x": (f // 2) % 4, "z": f // 8, "y": lax.axis_index("rows")}


def device(at):
    return (at["z"] * 8 + at["x"] * 2 + at["core"], at["y"])


def moved(at, axis, steps):
    there = dict(at)
    size = 2 if axis == "core" else 4
    there[axis] = (at[axis] + steps + size) % size
    return device(there)


def body(
    acts_hbm, grad_hbm, kern_hbm, gout, w16,
    acts, g, gt, k, a3, slope, w, r0, s1, r1, s2, r2, s3, r3,
    local_sem, halo_send, halo_recv, pair_send, pair_recv, ring_send, ring_recv,
):
    at = place()
    c = at["core"]
    f, r = lax.axis_index("frames"), lax.axis_index("rows")
    f_prev, f_next = (f + 31) % 32, (f + 1) % 32
    r_prev, r_next = (r + 3) % 4, (r + 1) % 4
    partner = moved(at, "core", 1)

    loads = [
        pltpu.make_async_copy(acts_hbm, acts, local_sem.at[0]),
        pltpu.make_async_copy(grad_hbm, g.at[pl.ds(0, 4), pl.ds(1, 3)], local_sem.at[1]),
        pltpu.make_async_copy(kern_hbm, k, local_sem.at[2]),
    ]
    for load in loads:
        load.start()

    barrier = pltpu.get_barrier_semaphore()
    peers = [partner, (f_prev, r), (f_next, r)]
    peers += [moved(at, axis, d) for axis in AXES for d in (1, 2, 3)]
    for peer in peers:
        pl.semaphore_signal(barrier, inc=1, device_id=peer, device_id_type=MESH)
    pl.semaphore_wait(barrier, len(peers))

    def remote(src, dst, ssem, rsem, to):
        return pltpu.make_async_remote_copy(
            src_ref=src, dst_ref=dst, send_sem=ssem, recv_sem=rsem,
            device_id=to, device_id_type=MESH,
        )

    def halo(n, src, dst, to):
        return remote(src, dst, halo_send.at[n], halo_recv.at[n], to)

    early, late, beyond = pl.ds(0, 2), pl.ds(2, 2), pl.ds(4, 2)
    halos = [
        halo(0, grad_hbm.at[early, 2], g.at[early, 0], (f, r_next)),
        halo(1, grad_hbm.at[early, 0], g.at[early, 4], (f, r_prev)),
        halo(2, grad_hbm.at[early], g.at[beyond, pl.ds(1, 3)], (f_prev, r)),
        halo(3, grad_hbm.at[late, 2], g.at[late, 0], (f, r_next)),
        halo(4, grad_hbm.at[late, 0], g.at[late, 4], (f, r_prev)),
        halo(5, g.at[early, 0], g.at[beyond, 0], (f_prev, r)),
        halo(6, g.at[early, 4], g.at[beyond, 4], (f_prev, r)),
    ]
    for copy in halos[:3]:
        copy.start()

    lane = lax.broadcasted_iota(jnp.int32, (256, 256), 1)

    def activate(t, h):
        x = acts[t, h].astype(F32)
        sig = jax.nn.sigmoid(x)
        activ = (x * sig).astype(BF16)
        slope[t, h] = sig * (1.0 + x * (1.0 - sig))
        wide = activ.astype(F32)
        a3[t, h, 1] = activ
        a3[t, h, 0] = jnp.where(lane == 0, 0.0, pltpu.roll(wide, 1, 1)).astype(BF16)
        a3[t, h, 2] = jnp.where(lane == 255, 0.0, pltpu.roll(wide, 255, 1)).astype(BF16)

    def turn(t, row):
        gt[t, row] = g[t, row].T

    HERE, ABOVE_BELOW, NEXT = range(3)

    def weight_part(n, parts, more=False):
        kt, kh = TAPS[n]
        acc = w[n].reshape(768, 256) if more else None
        for t in range(4):
            for h in range(3):
                frame, row = t + 2 - kt, h + 2 - kh
                part = NEXT if frame > 3 else HERE if 1 <= row <= 3 else ABOVE_BELOW
                if part not in parts:
                    continue
                term = jnp.dot(
                    a3[t, h].reshape(768, 256), gt[frame, row], preferred_element_type=F32
                )
                acc = term if acc is None else acc + term
        w[n] = acc.reshape(3, 256, 256)

    def input_grad(t, h):
        y = None
        for kt in range(3):
            for kh in range(3):
                term = jnp.dot(
                    k[kt, kh].reshape(768, 256), g[t + 2 - kt, h + 2 - kh],
                    preferred_element_type=F32,
                )
                y = term if y is None else y + term
        left = jnp.where(lane == 255, 0.0, pltpu.roll(y[:256], 255, 1))
        right = jnp.where(lane == 0, 0.0, pltpu.roll(y[512:], 1, 1))
        gout[t, h] = ((y[256:512] + left + right) * slope[t, h]).astype(BF16)

    loads[0].wait()
    loads[1].wait()

    @pl.loop(0, 4)
    def _(t):
        for h in range(3):
            activate(t, h)
            turn(t, h + 1)

    def clear(frames, row):
        for t in frames:
            g[t, row] = jnp.zeros((256, 256), BF16)

    def edge_rows(frames):
        @pl.when(r == 0)
        def _():
            clear(frames, 0)

        @pl.when(r == 3)
        def _():
            clear(frames, 4)

    def taps(batch):
        return pl.ds(*BATCHES[batch])

    def pair_sum(batch):
        return remote(
            w.at[taps(batch), :, pl.ds(pl.multiple_of(128 * (1 - c), 128), 128)],
            r0.at[taps(batch)], pair_send.at[batch], pair_recv.at[batch], partner,
        )

    def pair_gather(batch, half):
        part = w16.at[taps(batch), :, pl.ds(pl.multiple_of(128 * half, 128), 128)]
        n = len(BATCHES) + batch
        return remote(part, part, pair_send.at[n], pair_recv.at[n], partner)

    def ring(stage, batch, kw, d, src, dst, axis):
        n = ((stage * len(BATCHES) + batch) * 3 + kw) * 3 + d
        return remote(src, dst, ring_send.at[n], ring_recv.at[n], moved(at, axis, d + 1))

    def order(kw):
        return AXES[kw], AXES[(kw + 1) % 3], AXES[(kw + 2) % 3]

    def tile(p, base=0):
        return (
            pl.ds(pl.multiple_of(base + 16 * (p // 2), 16), 16),
            pl.ds(pl.multiple_of(128 * (p % 2), 128), 128),
        )

    def rows32(p, base=0):
        return pl.ds(pl.multiple_of(base + 32 * p, 32), 32)

    def scatter_one(batch, kw, d):
        first = order(kw)[0]
        to = (at[first] + d + 1) % 4
        return ring(
            0, batch, kw, d, s1.at[kw, taps(batch), rows32(to)], r1.at[kw, d, taps(batch)], first
        )

    def scatter_two(batch, kw, d):
        second = order(kw)[1]
        rows, cols = tile((at[second] + d + 1) % 4)
        return ring(
            1, batch, kw, d, s2.at[kw, taps(batch), rows, cols], r2.at[kw, d, taps(batch)], second
        )

    def sum_three(batch, kw, d):
        part = taps(batch)
        return ring(2, batch, kw, d, s3.at[kw, part], r3.at[kw, d, part], order(kw)[2])

    def gather_two(batch, kw, d, back=0):
        first, second, _ = order(kw)
        rows, cols = tile((at[second] + 4 - back) % 4, 128 * c + 32 * at[first])
        part = w16.at[taps(batch), kw, rows, cols]
        return ring(3, batch, kw, d, part, part, second)

    def gather_one(batch, kw, d, back=0):
        first = order(kw)[0]
        part = w16.at[taps(batch), kw, rows32((at[first] + 4 - back) % 4, 128 * c)]
        return ring(4, batch, kw, d, part, part, first)

    def each_tap(batch):
        first, count = BATCHES[batch]
        return range(first, first + count)

    def start_pair(batch):
        pair_sum(batch).start()

    def start_one(batch):
        pair_sum(batch).wait_recv()
        mine = pl.ds(pl.multiple_of(128 * c, 128), 128)
        for kw in range(3):
            for n in each_tap(batch):
                s1[kw, n] = (w[n, kw, mine] + r0[n, kw]).astype(BF16)
            for d in range(3):
                scatter_one(batch, kw, d).start()

    def start_two(batch):
        for kw in range(3):
            p = at[order(kw)[0]]
            for d in range(3):
                scatter_one(batch, kw, d).wait_recv()
            for n in each_tap(batch):
                total = w[n, kw, rows32(p, 128 * c)] + r0[n, kw, rows32(p)]
                for d in range(3):
                    total = total + r1[kw, d, n].astype(F32)
                s2[kw, n] = total
            for d in range(3):
                scatter_two(batch, kw, d).start()

    def start_three(batch):
        part = taps(batch)
        for kw in range(3):
            rows, cols = tile(at[order(kw)[1]])
            for d in range(3):
                scatter_two(batch, kw, d).wait_recv()
            total = s2[kw, part, rows, cols]
            for d in range(3):
                total = total + r2[kw, d, part]
            s3[kw, part] = total
            for d in range(3):
                sum_three(batch, kw, d).start()

    def start_gather_two(batch):
        part = taps(batch)
        for kw in range(3):
            first, second, _ = order(kw)
            rows, cols = tile(at[second], 128 * c + 32 * at[first])
            for d in range(3):
                sum_three(batch, kw, d).wait_recv()
            total = (s3[kw, part] + r3[kw, 1, part]) + (r3[kw, 0, part] + r3[kw, 2, part])
            w16[part, kw, rows, cols] = total.astype(BF16)
            for d in range(3):
                gather_two(batch, kw, d).start()

    def start_gather_one(batch):
        for kw in range(3):
            for d in range(3):
                gather_two(batch, kw, d, d + 1).wait_recv()
            for d in range(3):
                gather_one(batch, kw, d).start()

    def start_pair_gather(batch):
        for kw in range(3):
            for d in range(3):
                gather_one(batch, kw, d, d + 1).wait_recv()
        pair_gather(batch, c).start()

    def finish(batch):
        pair_gather(batch, 1 - c).wait_recv()

    halos[0].wait_send()
    halos[1].wait_send()
    halos[3].start()
    halos[4].start()
    halos[0].wait_recv()
    halos[1].wait_recv()
    edge_rows((0, 1))
    halos[5].start()
    halos[6].start()
    weight_part(0, (HERE,))
    for t in (0, 1):
        turn(t, 0)
        turn(t, 4)
    weight_part(3, (HERE,))
    weight_part(4, (HERE,))

    halos[2].wait_recv()

    @pl.when(f == 31)
    def _():
        for row in (1, 2, 3):
            clear((4, 5), row)

    for t in (4, 5):
        for row in (1, 2, 3):
            turn(t, row)
    weight_part(1, (HERE, NEXT))
    weight_part(2, (HERE, NEXT))
    start_pair(0)
    loads[2].wait()

    halos[3].wait_recv()
    halos[4].wait_recv()
    edge_rows((2, 3))
    for t in (2, 3):
        turn(t, 0)
        turn(t, 4)
    weight_part(3, (ABOVE_BELOW,), more=True)
    weight_part(4, (ABOVE_BELOW,), more=True)
    start_pair(1)
    start_one(0)
    halos[5].wait_recv()
    halos[6].wait_recv()

    @pl.when(f == 31)
    def _():
        for row in (0, 4):
            clear((4, 5), row)

    for t in (4, 5):
        turn(t, 0)
        turn(t, 4)
    everything = (HERE, ABOVE_BELOW, NEXT)
    weight_part(5, everything)
    weight_part(6, everything)
    start_pair(2)
    start_one(1)
    start_two(0)
    weight_part(7, everything)
    weight_part(8, everything)
    start_pair(3)
    start_one(2)
    start_two(1)
    start_three(0)

    chunks = [(t, h) for t in range(4) for h in range(3)]
    steps = (
        None, (start_one, 3), (start_two, 2), (start_three, 1), (start_gather_two, 0), None,
        (start_two, 3), (start_three, 2), (start_gather_two, 1), (start_gather_one, 0), None,
        (start_three, 3), (start_gather_two, 2), (start_gather_one, 1), (start_pair_gather, 0), None,
        (start_gather_two, 3), (start_gather_one, 2), (start_pair_gather, 1), (finish, 0), None,
        (start_gather_one, 3), (start_pair_gather, 2), (finish, 1), None, (finish, 2),
    )
    for step in steps:
        if step is None:
            input_grad(*chunks.pop(0))
            input_grad(*chunks.pop(0))
        else:
            step[0](step[1])
    start_pair_gather(3)
    finish(3)

    for copy in halos[2:]:
        copy.wait_send()
    for batch in range(len(BATCHES)):
        pair_sum(batch).wait_send()
        pair_gather(batch, c).wait_send()
        for kw in range(3):
            for d in range(3):
                for step in (scatter_one, scatter_two, sum_three, gather_two, gather_one):
                    step(batch, kw, d).wait_send()


def fused(acts, grad_out, kernel):
    flops = 4 * 27 * 256 * 256 * 3072
    dma = pltpu.SemaphoreType.DMA
    return pl.pallas_call(
        body,
        out_shape=(
            pltpu.VMEM(acts.shape, BF16),
            pltpu.VMEM((9, 3, 256, 256), BF16),
        ),
        in_specs=[pl.BlockSpec(memory_space=pl.ANY)] * 3,
        out_specs=(pl.BlockSpec(memory_space=pltpu.VMEM),) * 2,
        scratch_shapes=[
            pltpu.VMEM((4, 3, 256, 256), BF16),
            pltpu.VMEM((6, 5, 256, 256), BF16),
            pltpu.VMEM((6, 5, 256, 256), BF16),
            pltpu.VMEM((3, 3, 3, 256, 256), BF16),
            pltpu.VMEM((4, 3, 3, 256, 256), BF16),
            pltpu.VMEM((4, 3, 256, 256), F32),
            pltpu.VMEM((9, 3, 256, 256), F32),
            pltpu.VMEM((9, 3, 128, 256), F32),
            pltpu.VMEM((3, 9, 128, 256), BF16),
            pltpu.VMEM((3, 3, 9, 32, 256), BF16),
            pltpu.VMEM((3, 9, 32, 256), F32),
            pltpu.VMEM((3, 3, 9, 16, 128), F32),
            pltpu.VMEM((3, 9, 16, 128), F32),
            pltpu.VMEM((3, 3, 9, 16, 128), F32),
            dma((3,)),
            dma((7,)),
            dma((7,)),
            dma((2 * len(BATCHES),)),
            dma((2 * len(BATCHES),)),
            dma((45 * len(BATCHES),)),
            dma((45 * len(BATCHES),)),
        ],
        compiler_params=pltpu.CompilerParams(
            collective_id=0, has_side_effects=True, vmem_limit_bytes=58 * 2**20
        ),
        cost_estimate=pl.CostEstimate(flops=flops, bytes_accessed=16_000_000, transcendentals=0),
        name="conv_grads",
    )(acts, grad_out, kernel)


def write_body(scale, gout, w16, gacts_hbm, wgrad_hbm, wide, sems):
    copies = [pltpu.make_async_copy(gout, gacts_hbm, sems.at[len(TAPS)])]
    copies[0].start()
    for n, (kt, kh) in enumerate(TAPS):
        wide[n] = w16[n].astype(F32) * scale
        copies.append(pltpu.make_async_copy(wide.at[n], wgrad_hbm.at[kt, kh], sems.at[n]))
        copies[-1].start()
    for copy in copies:
        copy.wait()


def on_device(acts, grad_out, kernel):
    cells = 1
    for dim, axis in ((0, "frames"), (1, "rows")):
        cells *= acts.shape[dim] * lax.axis_size(axis)
    cells *= acts.shape[3]
    return pl.pallas_call(
        functools.partial(write_body, 1.0 / math.sqrt(cells)),
        out_shape=(
            jax.ShapeDtypeStruct(acts.shape, BF16),
            jax.ShapeDtypeStruct(kernel.shape, F32),
        ),
        in_specs=[pl.BlockSpec(memory_space=pltpu.VMEM)] * 2,
        out_specs=(pl.BlockSpec(memory_space=pl.ANY),) * 2,
        scratch_shapes=[
            pltpu.VMEM((9, 3, 256, 256), F32),
            pltpu.SemaphoreType.DMA((1 + len(TAPS),)),
        ],
        compiler_params=pltpu.CompilerParams(vmem_limit_bytes=16 * 2**20),
        name="write_out",
    )(*fused(acts, grad_out, kernel))


def solution(mesh):
    placed = (P("frames", "rows", None, None), P("frames", "rows", None, None), P())
    return jax.shard_map(
        on_device,
        mesh=mesh,
        in_specs=placed,
        out_specs=(P("frames", "rows", None, None), P()),
        check_vma=False,
    )
```

```python
import functools
import math

import jax
import jax.numpy as jnp
from jax import lax
from jax.experimental import pallas as pl
from jax.experimental.pallas import tpu as pltpu
from jax.sharding import PartitionSpec as P

MESH = pl.DeviceIdType.MESH
BF16, F32 = jnp.bfloat16, jnp.float32
AXES = "xyz"
TAPS = ((2, 1), (1, 1), (0, 1), (2, 0), (2, 2), (1, 0), (1, 2), (0, 0), (0, 2))
BATCHES = ((0, 3), (3, 2), (5, 4))
FAR_FIRST = (1, 0, 2)
LAST = len(BATCHES) - 1


def place():
    f = lax.axis_index("frames")
    return {"core": f % 2, "x": (f // 2) % 4, "z": f // 8, "y": lax.axis_index("rows")}


def device(at):
    return (at["z"] * 8 + at["x"] * 2 + at["core"], at["y"])


def moved(at, axis, steps):
    there = dict(at)
    size = 2 if axis == "core" else 4
    there[axis] = (at[axis] + steps + size) % size
    return device(there)


def body(
    acts_hbm, grad_hbm, kern_hbm, gout, w16,
    acts, g, gt, k, a3, slope, w, r0, s1, r1, s2, r2, s3, r3,
    local_sem, halo_send, halo_recv, pair_send, pair_recv, ring_send, ring_recv, cross_send, cross_recv,
):
    at = place()
    c = at["core"]
    f, r = lax.axis_index("frames"), lax.axis_index("rows")
    f_prev, f_next = (f + 31) % 32, (f + 1) % 32
    r_prev, r_next = (r + 3) % 4, (r + 1) % 4
    partner = moved(at, "core", 1)

    loads = [
        pltpu.make_async_copy(acts_hbm, acts, local_sem.at[0]),
        pltpu.make_async_copy(grad_hbm, g.at[pl.ds(0, 4), pl.ds(1, 3)], local_sem.at[1]),
        pltpu.make_async_copy(kern_hbm, k, local_sem.at[2]),
    ]
    for load in loads:
        load.start()

    barrier = pltpu.get_barrier_semaphore()
    peers = [partner, (f_prev, r), (f_next, r)]
    peers += [moved(at, axis, d) for axis in AXES for d in (1, 2, 3)]
    peers += [moved({**at, "core": 1 - c}, axis, d) for axis in AXES for d in (1, 2, 3)]
    for peer in peers:
        pl.semaphore_signal(barrier, inc=1, device_id=peer, device_id_type=MESH)
    pl.semaphore_wait(barrier, len(peers))

    def remote(src, dst, ssem, rsem, to):
        return pltpu.make_async_remote_copy(
            src_ref=src, dst_ref=dst, send_sem=ssem, recv_sem=rsem,
            device_id=to, device_id_type=MESH,
        )

    def halo(n, src, dst, to):
        return remote(src, dst, halo_send.at[n], halo_recv.at[n], to)

    early, late, beyond = pl.ds(0, 2), pl.ds(2, 2), pl.ds(4, 2)
    halos = [
        halo(0, grad_hbm.at[early, 2], g.at[early, 0], (f, r_next)),
        halo(1, grad_hbm.at[early, 0], g.at[early, 4], (f, r_prev)),
        halo(2, grad_hbm.at[early], g.at[beyond, pl.ds(1, 3)], (f_prev, r)),
        halo(3, grad_hbm.at[late, 2], g.at[late, 0], (f, r_next)),
        halo(4, grad_hbm.at[late, 0], g.at[late, 4], (f, r_prev)),
        halo(5, g.at[early, 0], g.at[beyond, 0], (f_prev, r)),
        halo(6, g.at[early, 4], g.at[beyond, 4], (f_prev, r)),
    ]
    for copy in halos[:3]:
        copy.start()

    lane = lax.broadcasted_iota(jnp.int32, (256, 256), 1)

    def activate(t, h):
        x = acts[t, h].astype(F32)
        sig = jax.nn.sigmoid(x)
        activ = (x * sig).astype(BF16)
        slope[t, h] = sig * (1.0 + x * (1.0 - sig))
        wide = activ.astype(F32)
        a3[t, h, 1] = activ
        a3[t, h, 0] = jnp.where(lane == 0, 0.0, pltpu.roll(wide, 1, 1)).astype(BF16)
        a3[t, h, 2] = jnp.where(lane == 255, 0.0, pltpu.roll(wide, 255, 1)).astype(BF16)

    def turn(t, row):
        gt[t, row] = g[t, row].T

    HERE, EDGE, NEXT, CORNER = range(4)

    def weight_part(n, parts, more=False):
        kt, kh = TAPS[n]
        acc = w[n].reshape(768, 256) if more else None
        for t in range(4):
            for h in range(3):
                frame, row = t + 2 - kt, h + 2 - kh
                part = (NEXT if frame > 3 else HERE) if 1 <= row <= 3 else (
                    CORNER if frame > 3 else EDGE
                )
                if part not in parts:
                    continue
                term = jnp.dot(
                    a3[t, h].reshape(768, 256), gt[frame, row], preferred_element_type=F32
                )
                acc = term if acc is None else acc + term
        w[n] = acc.reshape(3, 256, 256)

    def input_grad(t, h):
        y = None
        for kt in range(3):
            for kh in range(3):
                term = jnp.dot(
                    k[kt, kh].reshape(768, 256), g[t + 2 - kt, h + 2 - kh],
                    preferred_element_type=F32,
                )
                y = term if y is None else y + term
        left = jnp.where(lane == 255, 0.0, pltpu.roll(y[:256], 255, 1))
        right = jnp.where(lane == 0, 0.0, pltpu.roll(y[512:], 1, 1))
        gout[t, h] = ((y[256:512] + left + right) * slope[t, h]).astype(BF16)

    loads[0].wait()
    loads[1].wait()

    @pl.loop(0, 4)
    def _(t):
        for h in range(3):
            activate(t, h)
            turn(t, h + 1)

    def clear(frames, row):
        for t in frames:
            g[t, row] = jnp.zeros((256, 256), BF16)

    def edge_rows(frames):
        @pl.when(r == 0)
        def _():
            clear(frames, 0)

        @pl.when(r == 3)
        def _():
            clear(frames, 4)

    def taps(batch):
        return pl.ds(*BATCHES[batch])

    def pair_sum(batch, kw):
        n = batch * 3 + kw
        return remote(
            w.at[taps(batch), kw, pl.ds(pl.multiple_of(128 * (1 - c), 128), 128)],
            r0.at[taps(batch), kw], pair_send.at[n], pair_recv.at[n], partner,
        )

    def pair_gather(batch, kw, half):
        part = w16.at[taps(batch), kw, pl.ds(pl.multiple_of(128 * half, 128), 128)]
        n = (len(BATCHES) + batch) * 3 + kw
        return remote(part, part, pair_send.at[n], pair_recv.at[n], partner)

    def ring(stage, batch, kw, d, src, dst, axis):
        n = ((stage * len(BATCHES) + batch) * 3 + kw) * 3 + d
        return remote(src, dst, ring_send.at[n], ring_recv.at[n], moved(at, axis, d + 1))

    def order(kw):
        return AXES[kw], AXES[(kw + 1) % 3], AXES[(kw + 2) % 3]

    def tile(p, base=0):
        return (
            pl.ds(pl.multiple_of(base + 16 * (p // 2), 16), 16),
            pl.ds(pl.multiple_of(128 * (p % 2), 128), 128),
        )

    def rows32(p, base=0):
        return pl.ds(pl.multiple_of(base + 32 * p, 32), 32)

    def scatter_one(batch, kw, d):
        first = order(kw)[0]
        to = (at[first] + d + 1) % 4
        return ring(
            0, batch, kw, d, s1.at[kw, taps(batch), rows32(to)], r1.at[kw, d, taps(batch)], first
        )

    def scatter_two(batch, kw, d):
        second = order(kw)[1]
        rows, cols = tile((at[second] + d + 1) % 4)
        return ring(
            1, batch, kw, d, s2.at[kw, taps(batch), rows, cols], r2.at[kw, d, taps(batch)], second
        )

    def sum_three(batch, kw, d):
        part = taps(batch)
        return ring(2, batch, kw, d, s3.at[kw, part], r3.at[kw, d, part], order(kw)[2])

    def gather_two(batch, kw, d, back=0):
        first, second, _ = order(kw)
        rows, cols = tile((at[second] + 4 - back) % 4, 128 * c + 32 * at[first])
        part = w16.at[taps(batch), kw, rows, cols]
        return ring(3, batch, kw, d, part, part, second)

    def gather_one(batch, kw, d, back=0):
        first = order(kw)[0]
        part = w16.at[taps(batch), kw, rows32((at[first] + 4 - back) % 4, 128 * c)]
        return ring(4, batch, kw, d, part, part, first)

    def gather_cross(batch, kw, d, incoming=False):
        first = order(kw)[0]
        half, p = (1 - c, (at[first] + 3 - d) % 4) if incoming else (c, at[first])
        part = w16.at[taps(batch), kw, rows32(p, 128 * half)]
        n = kw * 4 + d
        to = moved({**at, "core": 1 - c}, first, d + 1)
        return remote(part, part, cross_send.at[n], cross_recv.at[n], to)

    def each_tap(batch):
        first, count = BATCHES[batch]
        return range(first, first + count)

    def start_pair(batch):
        for kw in range(3):
            pair_sum(batch, kw).start()

    def start_one(batch):
        mine = pl.ds(pl.multiple_of(128 * c, 128), 128)
        for kw in range(3):
            pair_sum(batch, kw).wait_recv()
            for n in each_tap(batch):
                s1[kw, n] = (w[n, kw, mine] + r0[n, kw]).astype(BF16)
            for d in FAR_FIRST:
                scatter_one(batch, kw, d).start()

    def start_two(batch):
        for kw in range(3):
            p = at[order(kw)[0]]
            for d in range(3):
                scatter_one(batch, kw, d).wait_recv()
            for n in each_tap(batch):
                total = w[n, kw, rows32(p, 128 * c)] + r0[n, kw, rows32(p)]
                for d in range(3):
                    total = total + r1[kw, d, n].astype(F32)
                s2[kw, n] = total
            for d in FAR_FIRST:
                scatter_two(batch, kw, d).start()

    def start_three(batch):
        part = taps(batch)
        for kw in range(3):
            rows, cols = tile(at[order(kw)[1]])
            for d in range(3):
                scatter_two(batch, kw, d).wait_recv()
            total = s2[kw, part, rows, cols]
            for d in range(3):
                total = total + r2[kw, d, part]
            s3[kw, part] = total
            for d in FAR_FIRST:
                sum_three(batch, kw, d).start()

    def start_gather_two(batch):
        part = taps(batch)
        for kw in range(3):
            first, second, _ = order(kw)
            rows, cols = tile(at[second], 128 * c + 32 * at[first])
            for d in range(3):
                sum_three(batch, kw, d).wait_recv()
            total = (s3[kw, part] + r3[kw, 1, part]) + (r3[kw, 0, part] + r3[kw, 2, part])
            w16[part, kw, rows, cols] = total.astype(BF16)
            for d in FAR_FIRST:
                gather_two(batch, kw, d).start()

    def start_gather_one(batch):
        for kw in range(3):
            for d in range(3):
                gather_two(batch, kw, d, d + 1).wait_recv()
            for d in FAR_FIRST:
                gather_one(batch, kw, d).start()
            if batch == LAST:
                for d in range(4):
                    gather_cross(batch, kw, d).start()

    def start_pair_gather(batch):
        for kw in range(3):
            for d in range(3):
                gather_one(batch, kw, d, d + 1).wait_recv()
            if batch == LAST:
                for d in range(4):
                    gather_cross(batch, kw, d, incoming=True).wait_recv()
            if batch != LAST:
                pair_gather(batch, kw, c).start()

    def finish(batch):
        if batch != LAST:
            for kw in range(3):
                pair_gather(batch, kw, 1 - c).wait_recv()

    weight_part(0, (HERE,))
    weight_part(3, (HERE,))

    halos[0].wait_send()
    halos[1].wait_send()
    halos[3].start()
    halos[4].start()
    halos[0].wait_recv()
    halos[1].wait_recv()
    edge_rows((0, 1))
    halos[5].start()
    halos[6].start()
    for n in (4, 1, 2, 5, 6, 7, 8):
        weight_part(n, (HERE,))

    halos[2].wait_recv()

    @pl.when(f == 31)
    def _():
        for row in (1, 2, 3):
            clear((4, 5), row)

    for t in (4, 5):
        for row in (1, 2, 3):
            turn(t, row)
    weight_part(1, (NEXT,), more=True)
    weight_part(2, (NEXT,), more=True)
    start_pair(0)

    halos[3].wait_recv()
    halos[4].wait_recv()
    edge_rows((2, 3))
    for t in range(4):
        turn(t, 0)
        turn(t, 4)
    weight_part(3, (EDGE,), more=True)
    weight_part(4, (EDGE,), more=True)
    start_pair(1)
    start_one(0)
    for n in (5, 6, 7, 8):
        weight_part(n, (EDGE, NEXT), more=True)
    start_one(1)

    halos[5].wait_recv()
    halos[6].wait_recv()

    @pl.when(f == 31)
    def _():
        for row in (0, 4):
            clear((4, 5), row)

    for t in (4, 5):
        turn(t, 0)
        turn(t, 4)
    weight_part(5, (CORNER,), more=True)
    weight_part(6, (CORNER,), more=True)
    weight_part(7, (CORNER,), more=True)
    weight_part(8, (CORNER,), more=True)
    start_pair(2)
    start_two(0)
    loads[2].wait()

    chunks = [(t, h) for t in range(4) for h in range(3)]
    steps = (
        None, (start_two, 1), (start_one, 2), None, (start_three, 0), None, None,
        (start_gather_two, 0), (start_three, 1), (start_two, 2), None, None,
        (start_gather_one, 0), (start_gather_two, 1), (start_three, 2), None, None,
        (start_pair_gather, 0), (start_gather_one, 1), (start_gather_two, 2), None, None,
        (start_pair_gather, 1), (start_gather_one, 2), None, None, (finish, 0),
        (start_pair_gather, 2), (finish, 1), (finish, 2),
    )
    for step in steps:
        if step is None:
            input_grad(*chunks.pop(0))
        else:
            step[0](step[1])

    for copy in halos[2:]:
        copy.wait_send()
    for batch in range(len(BATCHES)):
        for kw in range(3):
            pair_sum(batch, kw).wait_send()
            if batch != LAST:
                pair_gather(batch, kw, c).wait_send()
            for d in range(3):
                for step in (scatter_one, scatter_two, sum_three, gather_two, gather_one):
                    step(batch, kw, d).wait_send()
    for kw in range(3):
        for d in range(4):
            gather_cross(LAST, kw, d).wait_send()


def fused(acts, grad_out, kernel):
    flops = 4 * 27 * 256 * 256 * 3072
    dma = pltpu.SemaphoreType.DMA
    return pl.pallas_call(
        body,
        out_shape=(
            pltpu.VMEM(acts.shape, BF16),
            pltpu.VMEM((9, 3, 256, 256), BF16),
        ),
        in_specs=[pl.BlockSpec(memory_space=pl.ANY)] * 3,
        out_specs=(pl.BlockSpec(memory_space=pltpu.VMEM),) * 2,
        scratch_shapes=[
            pltpu.VMEM((4, 3, 256, 256), BF16),
            pltpu.VMEM((6, 5, 256, 256), BF16),
            pltpu.VMEM((6, 5, 256, 256), BF16),
            pltpu.VMEM((3, 3, 3, 256, 256), BF16),
            pltpu.VMEM((4, 3, 3, 256, 256), BF16),
            pltpu.VMEM((4, 3, 256, 256), F32),
            pltpu.VMEM((9, 3, 256, 256), F32),
            pltpu.VMEM((9, 3, 128, 256), F32),
            pltpu.VMEM((3, 9, 128, 256), BF16),
            pltpu.VMEM((3, 3, 9, 32, 256), BF16),
            pltpu.VMEM((3, 9, 32, 256), F32),
            pltpu.VMEM((3, 3, 9, 16, 128), F32),
            pltpu.VMEM((3, 9, 16, 128), F32),
            pltpu.VMEM((3, 3, 9, 16, 128), F32),
            dma((3,)),
            dma((7,)),
            dma((7,)),
            dma((6 * len(BATCHES),)),
            dma((6 * len(BATCHES),)),
            dma((45 * len(BATCHES),)),
            dma((45 * len(BATCHES),)),
            dma((12,)),
            dma((12,)),
        ],
        compiler_params=pltpu.CompilerParams(
            collective_id=0, has_side_effects=True, vmem_limit_bytes=58 * 2**20
        ),
        cost_estimate=pl.CostEstimate(flops=flops, bytes_accessed=16_000_000, transcendentals=0),
        name="conv_grads",
    )(acts, grad_out, kernel)


def write_body(scale, gout, w16, gacts_hbm, wgrad_hbm, wide, sems):
    copies = [pltpu.make_async_copy(gout, gacts_hbm, sems.at[len(TAPS)])]
    copies[0].start()
    for n, (kt, kh) in enumerate(TAPS):
        wide[n] = w16[n].astype(F32) * scale
        copies.append(pltpu.make_async_copy(wide.at[n], wgrad_hbm.at[kt, kh], sems.at[n]))
        copies[-1].start()
    for copy in copies:
        copy.wait()


def on_device(acts, grad_out, kernel):
    cells = 1
    for dim, axis in ((0, "frames"), (1, "rows")):
        cells *= acts.shape[dim] * lax.axis_size(axis)
    cells *= acts.shape[3]
    return pl.pallas_call(
        functools.partial(write_body, 1.0 / math.sqrt(cells)),
        out_shape=(
            jax.ShapeDtypeStruct(acts.shape, BF16),
            jax.ShapeDtypeStruct(kernel.shape, F32),
        ),
        in_specs=[pl.BlockSpec(memory_space=pltpu.VMEM)] * 2,
        out_specs=(pl.BlockSpec(memory_space=pl.ANY),) * 2,
        scratch_shapes=[
            pltpu.VMEM((9, 3, 256, 256), F32),
            pltpu.SemaphoreType.DMA((1 + len(TAPS),)),
        ],
        compiler_params=pltpu.CompilerParams(vmem_limit_bytes=16 * 2**20),
        name="write_out",
    )(*fused(acts, grad_out, kernel))


def solution(mesh):
    placed = (P("frames", "rows", None, None), P("frames", "rows", None, None), P())
    return jax.shard_map(
        on_device,
        mesh=mesh,
        in_specs=placed,
        out_specs=(P("frames", "rows", None, None), P()),
        check_vma=False,
    )
```

```python
import functools
import math

import jax
import jax.numpy as jnp
from jax import lax
from jax.experimental import pallas as pl
from jax.experimental.pallas import tpu as pltpu
from jax.sharding import PartitionSpec as P

MESH = pl.DeviceIdType.MESH
BF16, F32 = jnp.bfloat16, jnp.float32
AXES = "xyz"
TAPS = ((2, 1), (1, 1), (0, 1), (2, 0), (2, 2), (1, 0), (1, 2), (0, 0), (0, 2))
BATCHES = ((0, 3), (3, 2), (5, 4))
FAR_FIRST = (1, 0, 2)
LAST = len(BATCHES) - 1


def place():
    f = lax.axis_index("frames")
    return {"core": f % 2, "x": (f // 2) % 4, "z": f // 8, "y": lax.axis_index("rows")}


def device(at):
    return (at["z"] * 8 + at["x"] * 2 + at["core"], at["y"])


def moved(at, axis, steps):
    there = dict(at)
    size = 2 if axis == "core" else 4
    there[axis] = (at[axis] + steps + size) % size
    return device(there)


def body(
    acts_hbm, grad_hbm, kern_hbm, gout, w16,
    acts, g, gt, k, a3, slope, w, r0, s1, r1, s2, r2, s3, r3,
    local_sem, halo_send, halo_recv, pair_send, pair_recv, ring_send, ring_recv, cross_send, cross_recv,
):
    at = place()
    c = at["core"]
    f, r = lax.axis_index("frames"), lax.axis_index("rows")
    f_prev, f_next = (f + 31) % 32, (f + 1) % 32
    r_prev, r_next = (r + 3) % 4, (r + 1) % 4
    partner = moved(at, "core", 1)

    loads = [
        pltpu.make_async_copy(acts_hbm, acts, local_sem.at[0]),
        pltpu.make_async_copy(grad_hbm, g.at[pl.ds(0, 4), pl.ds(1, 3)], local_sem.at[1]),
        pltpu.make_async_copy(kern_hbm, k, local_sem.at[2]),
    ]
    for load in loads:
        load.start()

    barrier = pltpu.get_barrier_semaphore()
    peers = [partner, (f_prev, r), (f_next, r)]
    peers += [moved(at, axis, d) for axis in AXES for d in (1, 2, 3)]
    peers += [moved({**at, "core": 1 - c}, axis, d) for axis in AXES for d in (1, 2, 3)]
    for peer in peers:
        pl.semaphore_signal(barrier, inc=1, device_id=peer, device_id_type=MESH)
    pl.semaphore_wait(barrier, len(peers))

    def remote(src, dst, ssem, rsem, to):
        return pltpu.make_async_remote_copy(
            src_ref=src, dst_ref=dst, send_sem=ssem, recv_sem=rsem,
            device_id=to, device_id_type=MESH,
        )

    def halo(n, src, dst, to):
        return remote(src, dst, halo_send.at[n], halo_recv.at[n], to)

    early, late, beyond = pl.ds(0, 2), pl.ds(2, 2), pl.ds(4, 2)
    halos = [
        halo(0, grad_hbm.at[early, 2], g.at[early, 0], (f, r_next)),
        halo(1, grad_hbm.at[early, 0], g.at[early, 4], (f, r_prev)),
        halo(2, grad_hbm.at[early], g.at[beyond, pl.ds(1, 3)], (f_prev, r)),
        halo(3, grad_hbm.at[late, 2], g.at[late, 0], (f, r_next)),
        halo(4, grad_hbm.at[late, 0], g.at[late, 4], (f, r_prev)),
        halo(5, g.at[early, 0], g.at[beyond, 0], (f_prev, r)),
        halo(6, g.at[early, 4], g.at[beyond, 4], (f_prev, r)),
    ]
    for copy in halos[:3]:
        copy.start()

    lane = lax.broadcasted_iota(jnp.int32, (256, 256), 1)

    def activate(t, h):
        x = acts[t, h].astype(F32)
        sig = jax.nn.sigmoid(x)
        activ = (x * sig).astype(BF16)
        slope[t, h] = sig * (1.0 + x * (1.0 - sig))
        wide = activ.astype(F32)
        a3[t, h, 1] = activ
        a3[t, h, 0] = jnp.where(lane == 0, 0.0, pltpu.roll(wide, 1, 1)).astype(BF16)
        a3[t, h, 2] = jnp.where(lane == 255, 0.0, pltpu.roll(wide, 255, 1)).astype(BF16)

    def turn(t, row):
        gt[t, row] = g[t, row].T

    HERE, EDGE, NEXT, CORNER = range(4)

    def weight_part(n, parts, more=False):
        kt, kh = TAPS[n]
        acc = w[n].reshape(768, 256) if more else None
        for t in range(4):
            for h in range(3):
                frame, row = t + 2 - kt, h + 2 - kh
                part = (NEXT if frame > 3 else HERE) if 1 <= row <= 3 else (
                    CORNER if frame > 3 else EDGE
                )
                if part not in parts:
                    continue
                term = jnp.dot(
                    a3[t, h].reshape(768, 256), gt[frame, row], preferred_element_type=F32
                )
                acc = term if acc is None else acc + term
        w[n] = acc.reshape(3, 256, 256)

    def input_grad(t, h):
        y = None
        for kt in range(3):
            for kh in range(3):
                term = jnp.dot(
                    k[kt, kh].reshape(768, 256), g[t + 2 - kt, h + 2 - kh],
                    preferred_element_type=F32,
                )
                y = term if y is None else y + term
        left = jnp.where(lane == 255, 0.0, pltpu.roll(y[:256], 255, 1))
        right = jnp.where(lane == 0, 0.0, pltpu.roll(y[512:], 1, 1))
        gout[t, h] = ((y[256:512] + left + right) * slope[t, h]).astype(BF16)

    loads[0].wait()
    loads[1].wait()

    @pl.loop(0, 4)
    def _(t):
        for h in range(3):
            activate(t, h)
            turn(t, h + 1)

    def clear(frames, row):
        for t in frames:
            g[t, row] = jnp.zeros((256, 256), BF16)

    def edge_rows(frames):
        @pl.when(r == 0)
        def _():
            clear(frames, 0)

        @pl.when(r == 3)
        def _():
            clear(frames, 4)

    def taps(batch):
        return pl.ds(*BATCHES[batch])

    def pair_sum(batch, kw):
        n = batch * 3 + kw
        return remote(
            w.at[taps(batch), kw, pl.ds(pl.multiple_of(128 * (1 - c), 128), 128)],
            r0.at[taps(batch), kw], pair_send.at[n], pair_recv.at[n], partner,
        )

    def pair_gather(batch, kw, half):
        part = w16.at[taps(batch), kw, pl.ds(pl.multiple_of(128 * half, 128), 128)]
        n = (len(BATCHES) + batch) * 3 + kw
        return remote(part, part, pair_send.at[n], pair_recv.at[n], partner)

    def ring(stage, batch, kw, d, src, dst, axis):
        n = ((stage * len(BATCHES) + batch) * 3 + kw) * 3 + d
        return remote(src, dst, ring_send.at[n], ring_recv.at[n], moved(at, axis, d + 1))

    def order(kw):
        return AXES[kw], AXES[(kw + 1) % 3], AXES[(kw + 2) % 3]

    def tile(p, base=0):
        return (
            pl.ds(pl.multiple_of(base + 16 * (p // 2), 16), 16),
            pl.ds(pl.multiple_of(128 * (p % 2), 128), 128),
        )

    def rows32(p, base=0):
        return pl.ds(pl.multiple_of(base + 32 * p, 32), 32)

    def scatter_one(batch, kw, d):
        first = order(kw)[0]
        to = (at[first] + d + 1) % 4
        return ring(
            0, batch, kw, d, s1.at[kw, taps(batch), rows32(to)], r1.at[kw, d, taps(batch)], first
        )

    def scatter_two(batch, kw, d):
        second = order(kw)[1]
        rows, cols = tile((at[second] + d + 1) % 4)
        return ring(
            1, batch, kw, d, s2.at[kw, taps(batch), rows, cols], r2.at[kw, d, taps(batch)], second
        )

    def sum_three(batch, kw, d):
        part = taps(batch)
        return ring(2, batch, kw, d, s3.at[kw, part], r3.at[kw, d, part], order(kw)[2])

    def gather_two(batch, kw, d, back=0):
        first, second, _ = order(kw)
        rows, cols = tile((at[second] + 4 - back) % 4, 128 * c + 32 * at[first])
        part = w16.at[taps(batch), kw, rows, cols]
        return ring(3, batch, kw, d, part, part, second)

    def gather_one(batch, kw, d, back=0):
        first = order(kw)[0]
        part = w16.at[taps(batch), kw, rows32((at[first] + 4 - back) % 4, 128 * c)]
        return ring(4, batch, kw, d, part, part, first)

    def gather_cross(batch, kw, d, incoming=False):
        first = order(kw)[0]
        half, p = (1 - c, (at[first] + 3 - d) % 4) if incoming else (c, at[first])
        part = w16.at[taps(batch), kw, rows32(p, 128 * half)]
        n = kw * 4 + d
        to = moved({**at, "core": 1 - c}, first, d + 1)
        return remote(part, part, cross_send.at[n], cross_recv.at[n], to)

    def each_tap(batch):
        first, count = BATCHES[batch]
        return range(first, first + count)

    def start_pair(batch):
        for kw in range(3):
            pair_sum(batch, kw).start()

    def start_one(batch):
        mine = pl.ds(pl.multiple_of(128 * c, 128), 128)
        for kw in range(3):
            pair_sum(batch, kw).wait_recv()
            for n in each_tap(batch):
                s1[kw, n] = (w[n, kw, mine] + r0[n, kw]).astype(BF16)
            for d in FAR_FIRST:
                scatter_one(batch, kw, d).start()

    def start_two(batch):
        for kw in range(3):
            p = at[order(kw)[0]]
            for d in range(3):
                scatter_one(batch, kw, d).wait_recv()
            for n in each_tap(batch):
                total = w[n, kw, rows32(p, 128 * c)] + r0[n, kw, rows32(p)]
                for d in range(3):
                    total = total + r1[kw, d, n].astype(F32)
                s2[kw, n] = total
            for d in FAR_FIRST:
                scatter_two(batch, kw, d).start()

    def start_three(batch):
        part = taps(batch)
        for kw in range(3):
            rows, cols = tile(at[order(kw)[1]])
            for d in range(3):
                scatter_two(batch, kw, d).wait_recv()
            total = s2[kw, part, rows, cols]
            for d in range(3):
                total = total + r2[kw, d, part]
            s3[kw, part] = total
            for d in FAR_FIRST:
                sum_three(batch, kw, d).start()

    def start_gather_two(batch):
        part = taps(batch)
        for kw in range(3):
            first, second, _ = order(kw)
            rows, cols = tile(at[second], 128 * c + 32 * at[first])
            for d in range(3):
                sum_three(batch, kw, d).wait_recv()
            total = (s3[kw, part] + r3[kw, 1, part]) + (r3[kw, 0, part] + r3[kw, 2, part])
            w16[part, kw, rows, cols] = total.astype(BF16)
            for d in FAR_FIRST:
                gather_two(batch, kw, d).start()

    def start_gather_one(batch):
        for kw in range(3):
            for d in range(3):
                gather_two(batch, kw, d, d + 1).wait_recv()
            for d in FAR_FIRST:
                gather_one(batch, kw, d).start()
            if batch == LAST:
                for d in range(4):
                    gather_cross(batch, kw, d).start()

    def start_pair_gather(batch):
        for kw in range(3):
            for d in range(3):
                gather_one(batch, kw, d, d + 1).wait_recv()
            if batch == LAST:
                for d in range(4):
                    gather_cross(batch, kw, d, incoming=True).wait_recv()
            if batch != LAST:
                pair_gather(batch, kw, c).start()

    def finish(batch):
        if batch != LAST:
            for kw in range(3):
                pair_gather(batch, kw, 1 - c).wait_recv()

    weight_part(0, (HERE,))
    weight_part(3, (HERE,))

    halos[0].wait_send()
    halos[1].wait_send()
    halos[3].start()
    halos[4].start()
    halos[0].wait_recv()
    halos[1].wait_recv()
    edge_rows((0, 1))
    halos[5].start()
    halos[6].start()
    for n in (4, 1, 2, 5, 6, 7, 8):
        weight_part(n, (HERE,))

    halos[2].wait_recv()

    @pl.when(f == 31)
    def _():
        for row in (1, 2, 3):
            clear((4, 5), row)

    for t in (4, 5):
        for row in (1, 2, 3):
            turn(t, row)
    weight_part(1, (NEXT,), more=True)
    weight_part(2, (NEXT,), more=True)
    start_pair(0)

    halos[3].wait_recv()
    halos[4].wait_recv()
    edge_rows((2, 3))
    for t in range(4):
        turn(t, 0)
        turn(t, 4)
    weight_part(3, (EDGE,), more=True)
    weight_part(4, (EDGE,), more=True)
    start_pair(1)
    start_one(0)
    for n in (5, 6, 7, 8):
        weight_part(n, (EDGE, NEXT), more=True)
    start_one(1)

    halos[5].wait_recv()
    halos[6].wait_recv()

    @pl.when(f == 31)
    def _():
        for row in (0, 4):
            clear((4, 5), row)

    for t in (4, 5):
        turn(t, 0)
        turn(t, 4)
    weight_part(5, (CORNER,), more=True)
    weight_part(6, (CORNER,), more=True)
    weight_part(7, (CORNER,), more=True)
    weight_part(8, (CORNER,), more=True)
    start_pair(2)
    start_two(0)
    loads[2].wait()

    chunks = [(t, h) for t in range(4) for h in range(3)]
    steps = (
        (start_one, 2), None, (start_two, 1), (start_three, 0), None, None, (start_two, 2),
        (start_gather_two, 0), (start_three, 1), None, None, (start_three, 2),
        (start_gather_one, 0), (start_gather_two, 1), None, None, (start_gather_two, 2),
        (start_pair_gather, 0), (start_gather_one, 1), None, None, (start_gather_one, 2),
        (start_pair_gather, 1), None, None, None, (start_pair_gather, 2), (finish, 0),
        (finish, 1), (finish, 2),
    )
    for step in steps:
        if step is None:
            input_grad(*chunks.pop(0))
        else:
            step[0](step[1])

    for copy in halos[2:]:
        copy.wait_send()
    for batch in range(len(BATCHES)):
        for kw in range(3):
            pair_sum(batch, kw).wait_send()
            if batch != LAST:
                pair_gather(batch, kw, c).wait_send()
            for d in range(3):
                for step in (scatter_one, scatter_two, sum_three, gather_two, gather_one):
                    step(batch, kw, d).wait_send()
    for kw in range(3):
        for d in range(4):
            gather_cross(LAST, kw, d).wait_send()


def fused(acts, grad_out, kernel):
    flops = 4 * 27 * 256 * 256 * 3072
    dma = pltpu.SemaphoreType.DMA
    return pl.pallas_call(
        body,
        out_shape=(
            pltpu.VMEM(acts.shape, BF16),
            pltpu.VMEM((9, 3, 256, 256), BF16),
        ),
        in_specs=[pl.BlockSpec(memory_space=pl.ANY)] * 3,
        out_specs=(pl.BlockSpec(memory_space=pltpu.VMEM),) * 2,
        scratch_shapes=[
            pltpu.VMEM((4, 3, 256, 256), BF16),
            pltpu.VMEM((6, 5, 256, 256), BF16),
            pltpu.VMEM((6, 5, 256, 256), BF16),
            pltpu.VMEM((3, 3, 3, 256, 256), BF16),
            pltpu.VMEM((4, 3, 3, 256, 256), BF16),
            pltpu.VMEM((4, 3, 256, 256), F32),
            pltpu.VMEM((9, 3, 256, 256), F32),
            pltpu.VMEM((9, 3, 128, 256), F32),
            pltpu.VMEM((3, 9, 128, 256), BF16),
            pltpu.VMEM((3, 3, 9, 32, 256), BF16),
            pltpu.VMEM((3, 9, 32, 256), F32),
            pltpu.VMEM((3, 3, 9, 16, 128), F32),
            pltpu.VMEM((3, 9, 16, 128), F32),
            pltpu.VMEM((3, 3, 9, 16, 128), F32),
            dma((3,)),
            dma((7,)),
            dma((7,)),
            dma((6 * len(BATCHES),)),
            dma((6 * len(BATCHES),)),
            dma((45 * len(BATCHES),)),
            dma((45 * len(BATCHES),)),
            dma((12,)),
            dma((12,)),
        ],
        compiler_params=pltpu.CompilerParams(
            collective_id=0, has_side_effects=True, vmem_limit_bytes=58 * 2**20
        ),
        cost_estimate=pl.CostEstimate(flops=flops, bytes_accessed=16_000_000, transcendentals=0),
        name="conv_grads",
    )(acts, grad_out, kernel)


def write_body(scale, gout, w16, gacts_hbm, wgrad_hbm, wide, sems):
    copies = [pltpu.make_async_copy(gout, gacts_hbm, sems.at[len(TAPS)])]
    copies[0].start()
    for n, (kt, kh) in enumerate(TAPS):
        wide[n] = w16[n].astype(F32) * scale
        copies.append(pltpu.make_async_copy(wide.at[n], wgrad_hbm.at[kt, kh], sems.at[n]))
        copies[-1].start()
    for copy in copies:
        copy.wait()


def on_device(acts, grad_out, kernel):
    cells = 1
    for dim, axis in ((0, "frames"), (1, "rows")):
        cells *= acts.shape[dim] * lax.axis_size(axis)
    cells *= acts.shape[3]
    return pl.pallas_call(
        functools.partial(write_body, 1.0 / math.sqrt(cells)),
        out_shape=(
            jax.ShapeDtypeStruct(acts.shape, BF16),
            jax.ShapeDtypeStruct(kernel.shape, F32),
        ),
        in_specs=[pl.BlockSpec(memory_space=pltpu.VMEM)] * 2,
        out_specs=(pl.BlockSpec(memory_space=pl.ANY),) * 2,
        scratch_shapes=[
            pltpu.VMEM((9, 3, 256, 256), F32),
            pltpu.SemaphoreType.DMA((1 + len(TAPS),)),
        ],
        compiler_params=pltpu.CompilerParams(vmem_limit_bytes=16 * 2**20),
        name="write_out",
    )(*fused(acts, grad_out, kernel))


def solution(mesh):
    placed = (P("frames", "rows", None, None), P("frames", "rows", None, None), P())
    return jax.shard_map(
        on_device,
        mesh=mesh,
        in_specs=placed,
        out_specs=(P("frames", "rows", None, None), P()),
        check_vma=False,
    )
```
